32 devices in a mesh: groups: 2 (over y), uv: 4 (over z), chan: 2 (over x), pol: 2 (over core).
Axes of the slice: x: 2, y: 2, z: 4, core: 2. Of those that a mesh axis runs over, the one named last changes fastest.
Arguments:
- visibilities: bfloat16 [8, 256, 2, 128], P(('groups', 'chan', 'pol'), 'uv'), parts along dimension 0, may hold values from -6 to 6
- tile_pairs: int32 [512, 2, 128], P(('groups', 'uv')), parts along dimension 0, may hold values from 0 to 255
- owner_tiles: int32 [8, 256, 1], P(('groups', 'chan', 'pol'), 'uv'), parts along dimension 0, may hold values from 0 to 3; in each aligned block of 64 rows (0 to 63, 64 to 127, ..., all dimensions but the last counted through in order) at most 32 rows name the same one
- cell_ids: int32 [8, 256], P(('groups', 'chan', 'pol'), 'uv'), parts along dimension 0, may hold values from 0 to 255
- gains: float32 [8, 2, 256], P(('groups', 'chan', 'pol')), parts along dimension 0, may hold values from -4 to 4
- beams: float32 [256, 128], replicated, may hold values from -6 to 6
- support: int32 [256, 8], replicated, may hold values 0 or 1
Outputs:
- image: float32 [8, 2, 2048, 2048], P(('groups', 'chan', 'pol'), None, 'uv'), parts along dimension 0
The draws below stay inside these ranges and needn't reach their ends.
There are 2 independent parts, one for each index of `groups`. The reference program is written for one: setup_inputs(seed, part) draws one part's arguments, and reference() takes and returns one part's arrays. A program takes and returns all parts, laid end to end along the dimension named above; an argument that names none is the same for every part. Nothing has to cross between parts.
Inputs may be any that keep to these rules, and one draw needn't show every extreme that they name: `owner_tiles`: in each plane, the 64 blocks of one device along uv name no uv tile more than 32 times, a bound that some block reaches.
All inputs are finite; a program needn't handle non-finite values.
Results may differ from the reference program's by a relative error of at most 0.0052.
Values may be sent and summed in bfloat16 or wider, within the bound.
A program may use at most 128 MiB of HBM per device.

```python
import math
import jax
import jax.numpy as jnp
import numpy as np
from jax import lax

KERN = 64
GRID = 2048
ROWS = 128
TILES = 256
NBD = 64
PLANES = 4
NBLK = 256
MOST = 32
CPS = 256
N_UV = 4


def touch_ends(array, own_key, least, high):
    extent = array.shape
    spot = [jax.random.randint(jax.random.fold_in(own_key, axis), (), 0, extent[axis]) for axis in range(len(extent))]
    array = array.at[tuple(spot)].set(least)
    longest = extent.index(max(extent))
    spot[longest] = (spot[longest] + 1) % extent[longest]
    return array.at[tuple(spot)].set(high)


def steps_of(key, dims, split, smallest, largest):
    def one(position, blocks):
        heights = jax.random.uniform(jax.random.fold_in(jax.random.fold_in(key, 6), position), (blocks,), jnp.float32, smallest / len(split), largest / len(split))
        return jnp.repeat(jnp.exp(heights), dims[position] // blocks).reshape((-1,) + (1,) * (len(dims) - position - 1))

    loudness = one(*split[0])
    for cut in split[1:]:
        loudness = loudness * one(*cut)
    return loudness


def deal_out(rng, own, number, rows, number_of, top, reach, lean):
    order = jax.random.permutation(rng, number_of)
    packed, ordinary = load_shares(number_of, rows * top, reach, lean, True), load_shares(number_of, rows * top, reach, lean, False)
    places = jnp.arange(number_of)

    def named(lengths, rotation):
        used = int((lengths > 0).sum())
        fixed = max(1, used // 4)
        moved = fixed + (places - fixed + rotation * (used - fixed)) % max(1, number_of - fixed)
        return jnp.zeros((number_of,), jnp.int32).at[order[jnp.where(places < fixed, places, moved)]].set(jnp.asarray(lengths, jnp.int32))

    lengths = jnp.where(number % 4 == 0, named(packed, number // 4), named(ordinary, number - number // 4 - 1))
    mixed = jax.random.permutation(jax.random.fold_in(own, 3), number_of)
    giver, receiver = mixed[0:number_of // 2 * 2:2], mixed[1:number_of // 2 * 2:2]
    room = jnp.minimum(lengths[giver] - 1, reach - lengths[receiver]) // 2
    room = jnp.where((giver == order[0]) | (receiver == order[0]) | (lengths[receiver] == 0), 0, jnp.maximum(room, 0))
    moved = jax.random.randint(jax.random.fold_in(own, 4), (number_of // 2,), 0, 1 << 20) % (room + 1)
    lengths = lengths.at[giver].add(-moved).at[receiver].add(moved)
    members = jnp.searchsorted(jnp.cumsum(lengths), jnp.arange(rows * top), side="right").astype(jnp.int32)
    table = members.reshape(top, rows).T
    table = table[jax.random.permutation(jax.random.fold_in(own, 1), rows)]
    rotation = jax.random.randint(jax.random.fold_in(own, 2), (rows, 1), 0, top)
    return jnp.take_along_axis(table, (jnp.arange(top)[None, :] + rotation) % top, axis=1)


def load_shares(amount, total, reach, slope, full):
    weights = [(1 << 20) // math.isqrt(grade ** slope) + 1 for grade in range(1, amount + 1)]
    largest = reach if full else min(reach, max(-(-total // amount), total * weights[0] // sum(weights)))
    least = 1 if total - largest >= amount - 1 else 0
    counts, surplus = [largest] + [least] * (amount - 1), total - largest - least * (amount - 1)
    while surplus > 0:
        free = [i for i in range(1, amount) if counts[i] < largest] or [i for i in range(1, amount) if counts[i] < reach]
        mass, left = sum([weights[i] for i in free]), surplus
        for i in free:
            addition = min(reach - counts[i], max(1, left * weights[i] // mass), surplus)
            counts[i] = counts[i] + addition
            surplus = surplus - addition
    return np.array(counts)


def bell_draw(rng, shape, deviation, reach, shards=(), kind=jnp.bfloat16):
    array = jax.random.normal(rng, shape, jnp.float32) * deviation
    if len(shards) > 0:
        array = steps_of(rng, shape, shards, -0.22, 0.18) * array
    return jnp.clip(array, min=-reach, max=reach).astype(kind)


def setup_inputs(seed: int = 0, part: int = 0) -> dict:
    key_of = jax.random.split(jax.random.key(seed), 8)
    part_splits = jax.random.split(jax.random.fold_in(key_of[7], part), 8)
    visibilities = bell_draw(part_splits[0], (PLANES, NBLK, 2, ROWS), 1.0, 6.0, ((0, 4), (1, 4)))
    tile_pairs = touch_ends(jax.random.randint(part_splits[1], (NBLK, 2, ROWS), 0, TILES), jax.random.fold_in(part_splits[1], 1), 0, TILES - 1).astype(jnp.int32)
    owner_tiles_keys = jax.random.split(jax.random.fold_in(part_splits[2], 1), PLANES * NBLK // NBD)
    owner_tiles_turns = jax.random.permutation(jax.random.fold_in(part_splits[2], 3), PLANES * NBLK // NBD)
    owner_tiles = jax.vmap(lambda own, number: deal_out(jax.random.fold_in(part_splits[2], 2), own, number, NBD, N_UV, 1, MOST, 2))(owner_tiles_keys, owner_tiles_turns).reshape((PLANES, NBLK, 1))
    cell_ids = touch_ends(jax.random.randint(part_splits[3], (PLANES, NBLK), 0, CPS), jax.random.fold_in(part_splits[3], 1), 0, CPS - 1).astype(jnp.int32)
    gains = bell_draw(part_splits[4], (PLANES, 2, TILES), 0.7, 4.0, ((0, 4),), jnp.float32)
    beams = bell_draw(key_of[5], (TILES, 2 * KERN), 1.0, 6.0, (), jnp.float32)
    support = touch_ends((jax.random.randint(key_of[6], (TILES, 8), 0, 4) < 3).astype(jnp.int32), jax.random.fold_in(key_of[6], 1), 0, 1)
    return dict(visibilities=visibilities, tile_pairs=tile_pairs, owner_tiles=owner_tiles, cell_ids=cell_ids, gains=gains, beams=beams, support=support)


def kernel_table(beams, support):
    half_width = beams.shape[1] // 2
    band_width = half_width // 4
    mask_along_u = jnp.repeat(support[:, :4], band_width, axis=1)
    mask_along_v = jnp.repeat(support[:, 4:], band_width, axis=1)
    return beams * jnp.concatenate([mask_along_u, mask_along_v], axis=1).astype(jnp.float32)

def apply_gains(raw_blocks, first_tile, second_tile, plane_gains):
    gain_real = plane_gains[0]
    gain_imag = plane_gains[1]
    leading_real = jnp.take(gain_real, first_tile, axis=0)
    first_imag = jnp.take(gain_imag, first_tile, axis=0)
    second_real = jnp.take(gain_real, second_tile, axis=0)
    second_imag = jnp.take(gain_imag, second_tile, axis=0)
    visibility_real = raw_blocks[:, 0, :].astype(jnp.float32)
    vis_imag = raw_blocks[:, 1, :].astype(jnp.float32)
    prod_real = leading_real * visibility_real - first_imag * vis_imag
    prod_imag = leading_real * vis_imag + first_imag * visibility_real
    return (prod_real * second_real + prod_imag * second_imag, prod_imag * second_real - prod_real * second_imag)

def grid_blocks(visibility_real, vis_imag, first_tile, second_tile, beam_table):
    half_width = beam_table.shape[1] // 2
    convolution_kernels = jnp.take(beam_table, first_tile, axis=0) * jnp.take(beam_table, second_tile, axis=0)
    along_u = convolution_kernels[..., :half_width]
    along_v = convolution_kernels[..., half_width:]
    weighted = jnp.concatenate([visibility_real[..., None] * along_v, vis_imag[..., None] * along_v], axis=-1)
    return jnp.einsum('gra,grx->gax', along_u, weighted, precision=lax.Precision.HIGHEST)

def dft_tables(offset, block_width, total):
    row_index = offset + jnp.arange(block_width, dtype=jnp.int32)
    col_index = jnp.arange(total, dtype=jnp.int32)
    products = row_index[:, None] * col_index[None, :] % total
    angles = products.astype(jnp.float32) * (2.0 * math.pi / total)
    return (jnp.cos(angles).astype(jnp.bfloat16), jnp.sin(angles).astype(jnp.bfloat16))

def precise_dot(left, right):
    return jnp.dot(left, right, precision=lax.Precision.HIGHEST, preferred_element_type=jnp.float32)

def reference(visibilities, tile_pairs, owner_tiles, cell_ids, gains, beams, support):
    beam_table = kernel_table(beams, support)
    first_tile = tile_pairs[:, 0, :]
    second_tile = tile_pairs[:, 1, :]
    strip_rows = GRID // N_UV
    columns = GRID // KERN
    band_total = GRID // KERN
    cos_table, sin_table = dft_tables(0, GRID, GRID)
    cos_full = cos_table.astype(jnp.float32)
    sin_full = sin_table.astype(jnp.float32)
    scale_first = 1.0 / (16.0 * math.sqrt(GRID))
    scale_second = 1.0 / math.sqrt(GRID)
    nblocks = first_tile.shape[0]
    rows_each = first_tile.shape[1]

    def one_plane(plane_arguments):
        raw_blocks, owner_ids, cell_list, plane_gains = plane_arguments
        visibility_real, vis_imag = apply_gains(raw_blocks, first_tile, second_tile, plane_gains)

        def grid_group(pieces):
            return grid_blocks(pieces[0], pieces[1], pieces[2], pieces[3], beam_table)
        grouped = (visibility_real.reshape(N_UV, nblocks // N_UV, rows_each), vis_imag.reshape(N_UV, nblocks // N_UV, rows_each), first_tile.reshape(N_UV, nblocks // N_UV, rows_each), second_tile.reshape(N_UV, nblocks // N_UV, rows_each))
        subgrids = lax.map(grid_group, grouped).reshape(nblocks, KERN, 2 * KERN)
        band_ids = owner_ids * (strip_rows // KERN) + cell_list // columns
        col_ids = cell_list % columns
        uv_plane = jnp.zeros((band_total, columns, KERN, 2 * KERN), jnp.float32).at[band_ids, col_ids].add(subgrids)
        uv_plane = uv_plane.reshape(band_total, columns, KERN, 2, KERN).transpose(3, 0, 2, 1, 4).reshape(2, GRID, GRID)
        rounded = lax.optimization_barrier(uv_plane.astype(jnp.bfloat16)).astype(jnp.float32)
        plane_real = rounded[0]
        plane_imag = rounded[1]
        half_real = (precise_dot(plane_real, cos_full) - precise_dot(plane_imag, sin_full)).T * scale_first
        half_imag = (precise_dot(plane_real, sin_full) + precise_dot(plane_imag, cos_full)).T * scale_first
        half_real = lax.optimization_barrier(half_real.astype(jnp.bfloat16)).astype(jnp.float32)
        half_imag = lax.optimization_barrier(half_imag.astype(jnp.bfloat16)).astype(jnp.float32)
        image_real = (precise_dot(half_real, cos_full) - precise_dot(half_imag, sin_full)) * scale_second
        image_imag = (precise_dot(half_real, sin_full) + precise_dot(half_imag, cos_full)) * scale_second
        return jnp.stack([image_real, image_imag])
    return lax.map(one_plane, (visibilities, owner_tiles[:, :, 0], cell_ids, gains))
```

```python
import functools
import math

import jax
import jax.numpy as jnp
import ml_dtypes
import numpy as np
from jax import lax
from jax.experimental import pallas as pl
from jax.experimental.pallas import tpu as pltpu
from jax.sharding import PartitionSpec as P

GRID = 2048
KERN = 64
COLS = GRID // KERN
QUAD = 4
BATCH = 8
LIMIT = 60 * 1024 * 1024
BF = jnp.bfloat16
F32 = jnp.float32


@functools.lru_cache(maxsize=None)
def full_tables():
    index = np.arange(GRID)
    angles = 2.0 * np.pi * ((index[:, None] * index[None, :]) % GRID) / GRID
    return (
        np.cos(angles).astype(np.float32).astype(ml_dtypes.bfloat16),
        np.sin(angles).astype(np.float32).astype(ml_dtypes.bfloat16),
    )


@functools.lru_cache(maxsize=None)
def quad_table():
    cos_table, sin_table = full_tables()
    quarter = GRID // QUAD
    rows = np.arange(GRID).reshape(COLS, KERN // QUAD, QUAD)
    out = np.zeros((QUAD, COLS, 2, KERN // QUAD, 2, quarter), ml_dtypes.bfloat16)
    for r in range(QUAD):
        c = cos_table[rows[:, :, r], :quarter]
        s = sin_table[rows[:, :, r], :quarter]
        out[r, :, 0, :, 0] = c
        out[r, :, 1, :, 0] = -s
        out[r, :, 0, :, 1] = s
        out[r, :, 1, :, 1] = c
    return out.reshape(QUAD, GRID // 2, GRID // 2)


def grid_kernel(steps, place_ref, vis_ref, pair_ref, table_ref, plane_ref, total):
    step = pl.program_id(0)

    @pl.when(step == 0)
    def _():
        @pl.loop(0, COLS)
        def _(col):
            total[col] = jnp.zeros((COLS, KERN, 2 * KERN), F32)

    @pl.when(step < steps)
    def _():
        tiles = table_ref.shape[1]
        tile_number = lax.broadcasted_iota(jnp.int32, (tiles, 256), 0)
        table = table_ref[...]
        for j in range(BATCH):
            pair = jnp.concatenate(
                [pair_ref[2 * j : 2 * j + 1, :], pair_ref[2 * j + 1 : 2 * j + 2, :]], axis=1
            )
            chosen = jnp.where(tile_number == pair, 1.0, 0.0).astype(BF)
            rows = jnp.dot(table, chosen, preferred_element_type=F32)
            both = rows[:128] + rows[128:256]
            kernels = both[:, :128] * both[:, 128:]
            ku, kv = kernels[:64], kernels[64:]
            real = rows[256:257] + rows[257:258] + rows[258:259]
            imag = rows[259:260] + rows[260:261] + rows[261:262]
            sr, tr, si, ti = real[:, :128], real[:, 128:], imag[:, :128], imag[:, 128:]
            vr, vi = vis_ref[2 * j : 2 * j + 1, :], vis_ref[2 * j + 1 : 2 * j + 2, :]
            pr = sr * vr - si * vi
            pi = sr * vi + si * vr
            gr = pr * tr + pi * ti
            gi = pi * tr - pr * ti
            weighted = []
            for r in range(QUAD):
                band = ku[16 * r : 16 * r + 16]
                weighted += [gr * band, gi * band]
            weighted = jnp.concatenate(weighted, axis=0)
            w_high = weighted.astype(BF)
            w_low = (weighted - w_high.astype(F32)).astype(BF)
            v_high = kv.astype(BF)
            v_low = (kv - v_high.astype(F32)).astype(BF)
            product = lax.dot_general(
                jnp.concatenate([v_high, v_low], axis=0),
                jnp.concatenate([w_high, w_low], axis=0),
                (((1,), (1,)), ((), ())),
                preferred_element_type=F32,
            )
            cell = product[:64, :128] + (
                product[64:, :128] + product[:64, 128:] + product[64:, 128:]
            )
            where = place_ref[step * BATCH + j]
            total[where // COLS, where % COLS] += cell

    @pl.when(step >= steps)
    def _():
        first = (step - steps) * 2

        for half in range(2):
            for row in range(COLS):
                plane_ref[half * KERN : (half + 1) * KERN, row * 128 : (row + 1) * 128] = total[
                    first + half, row
                ].astype(BF)


def grid_plane(places, vis, pairs, table):
    nblocks = places.shape[0]
    steps = nblocks // BATCH
    rows = table.shape[0]
    tiles = table.shape[1]
    return pl.pallas_call(
        functools.partial(grid_kernel, steps),
        out_shape=jax.ShapeDtypeStruct((GRID, 2 * GRID), BF),
        grid_spec=pltpu.PrefetchScalarGridSpec(
            num_scalar_prefetch=1,
            grid=(steps + COLS // 2,),
            in_specs=[
                pl.BlockSpec((2 * BATCH, 128), lambda i, p: (jnp.minimum(i, steps - 1), 0)),
                pl.BlockSpec((2 * BATCH, 128), lambda i, p: (jnp.minimum(i, steps - 1), 0)),
                pl.BlockSpec((rows, tiles), lambda i, p: (0, 0)),
            ],
            out_specs=pl.BlockSpec((128, 2 * GRID), lambda i, p: (jnp.maximum(i - steps, 0), 0)),
            scratch_shapes=[pltpu.VMEM((COLS, COLS, KERN, 2 * KERN), F32)],
        ),
        compiler_params=pltpu.CompilerParams(vmem_limit_bytes=LIMIT),
    )(places, vis, pairs, table)


def image_kernel(band, tile, me_ref, cos_ref, sin_ref, plane_ref, quad_ref, image_ref, spectrum):
    step = pl.program_id(0)
    groups = COLS // 4
    scale_first = 1.0 / (16.0 * math.sqrt(GRID))
    scale_second = 1.0 / math.sqrt(GRID)
    quarter = GRID // QUAD

    @pl.when(step < groups)
    def _():
        data = plane_ref[...]
        lane = lax.broadcasted_iota(jnp.int32, (tile, 512), 1) % 32
        for top in range(0, band, tile):
            with_cos = jnp.dot(cos_ref[top : top + tile, :], data, preferred_element_type=F32)
            with_sin = jnp.dot(sin_ref[top : top + tile, :], data, preferred_element_type=F32)
            swapped = jnp.where(
                lane < 16, -pltpu.roll(with_sin, 512 - 16, 1), pltpu.roll(with_sin, 16, 1)
            )
            mixed = (with_cos + swapped) * scale_first
            for r in range(QUAD):
                picked = jnp.concatenate(
                    [mixed[:, 128 * k + 32 * r : 128 * k + 32 * r + 32] for k in range(4)], axis=1
                )
                spectrum[r, top : top + tile, pl.ds(pl.multiple_of(step * 128, 128), 128)] = (
                    picked.astype(BF)
                )

    @pl.when(step >= groups)
    def _():
        top = pl.multiple_of((step - groups) * tile, tile)
        for left in range(0, quarter, 256):
            real, imag = [], []
            for r in range(QUAD):
                part = spectrum[r, pl.ds(top, tile), :]
                real.append(
                    jnp.dot(part, quad_ref[r, :, left : left + 256], preferred_element_type=F32)
                )
                imag.append(
                    jnp.dot(
                        part,
                        quad_ref[r, :, quarter + left : quarter + left + 256],
                        preferred_element_type=F32,
                    )
                )
            er, ei = real[0] + real[2], imag[0] + imag[2]
            fr, fi = real[0] - real[2], imag[0] - imag[2]
            gr, gi = real[1] + real[3], imag[1] + imag[3]
            hr, hi = real[1] - real[3], imag[1] - imag[3]
            parts = [
                (er + gr, ei + gi),
                (fr - hi, fi + hr),
                (er - gr, ei - gi),
                (fr + hi, fi - hr),
            ]
            for q in range(QUAD):
                at = q * quarter + left
                image_ref[0, 0, :, at : at + 256] = parts[q][0] * scale_second
                image_ref[0, 1, :, at : at + 256] = parts[q][1] * scale_second


def make_image(me, plane, band):
    cos_table, sin_table = full_tables()
    tile = min(256, band)
    groups = COLS // 4
    return pl.pallas_call(
        functools.partial(image_kernel, band, tile),
        out_shape=jax.ShapeDtypeStruct((1, 2, band, GRID), F32),
        grid_spec=pltpu.PrefetchScalarGridSpec(
            num_scalar_prefetch=1,
            grid=(groups + band // tile,),
            in_specs=[
                pl.BlockSpec((band, GRID), lambda i, m: (m[0], 0)),
                pl.BlockSpec((band, GRID), lambda i, m: (m[0], 0)),
                pl.BlockSpec((GRID, 512), lambda i, m: (0, jnp.minimum(i, groups - 1))),
                pl.BlockSpec((QUAD, GRID // 2, GRID // 2), lambda i, m: (0, 0, 0)),
            ],
            out_specs=pl.BlockSpec(
                (1, 2, tile, GRID), lambda i, m: (0, 0, jnp.maximum(i - groups, 0), 0)
            ),
            scratch_shapes=[pltpu.VMEM((QUAD, band, GRID // 2), BF)],
        ),
        compiler_params=pltpu.CompilerParams(vmem_limit_bytes=LIMIT),
    )(me, jnp.asarray(cos_table), jnp.asarray(sin_table), plane, jnp.asarray(quad_table()))


def rounded(x):
    return lax.reduce_precision(x, exponent_bits=8, mantissa_bits=7)


def lookup_rows(beams, support, gains):
    half = beams.shape[1] // 2
    width = half // 4
    masked = beams * jnp.repeat(support, width, axis=1).astype(F32)
    by_column = masked.T
    along_u = by_column[:half].reshape(half // QUAD, QUAD, -1).transpose(1, 0, 2).reshape(half, -1)
    values = jnp.concatenate([along_u, by_column[half:]], axis=0)
    high = rounded(values)
    low = values - high
    gain_high = rounded(gains)
    rest = gains - gain_high
    gain_mid = rounded(rest)
    gain_low = rest - gain_mid
    gain_rows = jnp.stack([gain_high, gain_mid, gain_low], axis=1).reshape(6, -1)
    blank = jnp.zeros((10, gains.shape[1]), F32)
    return jnp.concatenate([high, low, gain_rows, blank], axis=0).astype(BF)


def on_device(visibilities, tile_pairs, owner_tiles, cell_ids, gains, beams, support):
    owners = lax.axis_size("uv")
    me = lax.axis_index("uv").astype(jnp.int32).reshape(1)
    nblocks, _, rows_each = visibilities.shape[1:]
    band = GRID // owners
    bands_each = band // KERN
    lines = 2 * nblocks * rows_each // 128
    meta = jnp.concatenate([owner_tiles[0, :, 0], cell_ids[0]]).reshape(-1, 128)
    meta = jnp.pad(meta, ((0, 16 - meta.shape[0]), (0, 0)))
    packed = jnp.concatenate(
        [
            visibilities.reshape(lines, 128),
            tile_pairs.reshape(lines, 128).astype(BF),
            meta.astype(BF),
        ],
        axis=0,
    )
    gathered = lax.all_gather(packed, "uv", axis=0, tiled=False)
    vis = gathered[:, :lines].reshape(owners * lines, 128).astype(F32)
    pairs = gathered[:, lines : 2 * lines].reshape(owners * lines, 128).astype(jnp.int32)
    notes = gathered[:, 2 * lines : 2 * lines + 2 * nblocks // 128].reshape(owners, 2, nblocks)
    notes = notes.astype(jnp.int32)
    cells = notes[:, 1]
    places = (cells % COLS) * COLS + notes[:, 0] * bands_each + cells // COLS
    table = lookup_rows(beams, support, gains[0])
    plane = grid_plane(places.reshape(-1), vis, pairs, table)
    return make_image(me, plane, band)


def solution(mesh):
    return jax.shard_map(
        on_device,
        mesh=mesh,
        in_specs=(
            P(("groups", "chan", "pol"), "uv", None, None),
            P(("groups", "uv"), None, None),
            P(("groups", "chan", "pol"), "uv", None),
            P(("groups", "chan", "pol"), "uv"),
            P(("groups", "chan", "pol"), None, None),
            P(),
            P(),
        ),
        out_specs=P(("groups", "chan", "pol"), None, "uv", None),
        check_vma=False,
    )
```

```python
import functools
import math

import jax
import jax.numpy as jnp
import ml_dtypes
import numpy as np
from jax import lax
from jax.experimental import pallas as pl
from jax.experimental.pallas import tpu as pltpu
from jax.sharding import PartitionSpec as P

GRID = 2048
KERN = 64
COLS = GRID // KERN
QUAD = 4
BATCH = 16
LIMIT = 60 * 1024 * 1024
BF = jnp.bfloat16
F32 = jnp.float32


@functools.lru_cache(maxsize=None)
def full_tables():
    index = np.arange(GRID)
    angles = 2.0 * np.pi * ((index[:, None] * index[None, :]) % GRID) / GRID
    return (
        np.cos(angles).astype(np.float32).astype(ml_dtypes.bfloat16),
        np.sin(angles).astype(np.float32).astype(ml_dtypes.bfloat16),
    )


@functools.lru_cache(maxsize=None)
def quad_table():
    cos_table, sin_table = full_tables()
    quarter = GRID // QUAD
    rows = np.arange(GRID).reshape(COLS, KERN // QUAD, QUAD)
    out = np.zeros((QUAD, COLS, 2, KERN // QUAD, 2, quarter), ml_dtypes.bfloat16)
    for r in range(QUAD):
        c = cos_table[rows[:, :, r], :quarter]
        s = sin_table[rows[:, :, r], :quarter]
        out[r, :, 0, :, 0] = c
        out[r, :, 1, :, 0] = -s
        out[r, :, 0, :, 1] = s
        out[r, :, 1, :, 1] = c
    return out.reshape(QUAD, GRID // 2, GRID // 2)


@functools.lru_cache(maxsize=None)
def class_tables(owners):
    cos_table, sin_table = full_tables()
    band = GRID // owners
    order = np.arange(GRID).reshape(owners, band // QUAD, QUAD).transpose(0, 2, 1).reshape(-1)
    quarter = GRID // QUAD
    return cos_table[order, :quarter], sin_table[order, :quarter]


def fused_kernel(
    band, tile, steps,
    place_ref, me_ref, vis_ref, pair_ref, table_ref, cos_ref, sin_ref, quad_hbm,
    image_ref,
    total, chosen, looked, left_rows, right_rows, mixed_cells, woven, spectrum, quad_ref, quad_sem,
):
    step = pl.program_id(0)
    groups = COLS // 4
    quarter = GRID // QUAD
    class_rows = band // QUAD
    scale_first = 1.0 / (16.0 * math.sqrt(GRID))
    scale_second = 1.0 / math.sqrt(GRID)
    quad_copy = pltpu.make_async_copy(quad_hbm, quad_ref, quad_sem)

    @pl.when(step == 0)
    def _():
        quad_copy.start()

        @pl.loop(0, COLS)
        def _(col):
            total[col] = jnp.zeros((COLS, KERN, 2 * KERN), F32)

    @pl.when(step < steps)
    def _():
        tiles = table_ref.shape[1]
        number = lax.broadcasted_iota(jnp.int32, (tiles, 256), 0).astype(F32).astype(BF)
        one, nil = jnp.asarray(1, BF), jnp.asarray(0, BF)
        for j in range(BATCH):
            pair = jnp.concatenate(
                [pair_ref[2 * j : 2 * j + 1, :], pair_ref[2 * j + 1 : 2 * j + 2, :]], axis=1
            )
            pair = jnp.broadcast_to(pair, (16, 256)).astype(BF)
            pair = jnp.concatenate([pair] * (tiles // 16), axis=0)
            chosen[:, j * 256 : (j + 1) * 256] = jnp.where(number == pair, one, nil)
        for j in range(0, BATCH, 2):
            looked[:, j * 256 : (j + 2) * 256] = jnp.dot(
                table_ref[...], chosen[:, j * 256 : (j + 2) * 256], preferred_element_type=F32
            )
        for j in range(BATCH):
            rows = looked[:, j * 256 : (j + 1) * 256]
            both = rows[:128] + rows[128:256]
            kernels = both[:, :128] * both[:, 128:]
            ku, kv = kernels[:64], kernels[64:]
            real = rows[256:257] + rows[257:258] + rows[258:259]
            imag = rows[259:260] + rows[260:261] + rows[261:262]
            sr, tr, si, ti = real[:, :128], real[:, 128:], imag[:, :128], imag[:, 128:]
            vr, vi = vis_ref[2 * j : 2 * j + 1, :], vis_ref[2 * j + 1 : 2 * j + 2, :]
            pr = sr * vr - si * vi
            pi = sr * vi + si * vr
            gr = pr * tr + pi * ti
            gi = pi * tr - pr * ti
            weighted = []
            for r in range(QUAD):
                part = ku[16 * r : 16 * r + 16]
                weighted += [gr * part, gi * part]
            weighted = jnp.concatenate(weighted, axis=0)
            w_high = weighted.astype(BF)
            w_low = (weighted - w_high.astype(F32)).astype(BF)
            v_high = kv.astype(BF)
            v_low = (kv - v_high.astype(F32)).astype(BF)
            left_rows[j] = jnp.concatenate([v_high, v_low], axis=0)
            right_rows[j] = jnp.concatenate([w_high, w_low], axis=0)
        for j in range(BATCH):
            product = lax.dot_general(
                left_rows[j], right_rows[j], (((1,), (1,)), ((), ())), preferred_element_type=F32
            )
            cell = product[:64, :128] + (
                product[64:, :128] + product[:64, 128:] + product[64:, 128:]
            )
            where = place_ref[step * BATCH + j]
            total[where // COLS, where % COLS] += cell

    @pl.when(step == steps)
    def _():
        quad_copy.wait()

    @pl.when((step >= steps) & (step < steps + groups))
    def _():
        group = step - steps
        far = COLS // QUAD

        @pl.loop(0, far)
        def _(col):
            top = pl.multiple_of(col * KERN, KERN)
            lane = lax.broadcasted_iota(jnp.int32, (KERN, 128), 1) % 32
            for k in range(4):
                x = [
                    total[col + far * q, group * 4 + k].astype(BF).astype(F32) for q in range(QUAD)
                ]
                e, f, g, h = x[0] + x[2], x[0] - x[2], x[1] + x[3], x[1] - x[3]
                turned = jnp.where(lane < 16, -pltpu.roll(h, 112, 1), pltpu.roll(h, 16, 1))
                for s, y in enumerate([e + g, f + turned, e - g, f - turned]):
                    mixed_cells[s, pl.ds(top, KERN), k * 128 : (k + 1) * 128] = y.astype(BF)

        lane = lax.broadcasted_iota(jnp.int32, (class_rows, 512), 1) % 32
        for s in range(QUAD):
            mine = slice(s * class_rows, (s + 1) * class_rows)
            data = mixed_cells[s]
            with_cos = jnp.dot(cos_ref[mine, :], data, preferred_element_type=F32)
            with_sin = jnp.dot(sin_ref[mine, :], data, preferred_element_type=F32)
            swapped = jnp.where(
                lane < 16, -pltpu.roll(with_sin, 512 - 16, 1), pltpu.roll(with_sin, 16, 1)
            )
            mixed = (with_cos + swapped) * scale_first
            for r in range(QUAD):
                picked = jnp.concatenate(
                    [mixed[:, 128 * k + 32 * r : 128 * k + 32 * r + 32] for k in range(4)], axis=1
                )
                woven[r, pl.ds(s, class_rows, stride=QUAD), :] = picked
        for r in range(QUAD):
            spectrum[r, :, pl.ds(pl.multiple_of(group * 128, 128), 128)] = woven[r].astype(BF)

    @pl.when(step >= steps + groups)
    def _():
        top = pl.multiple_of((step - steps - groups) * tile, tile)
        for left in range(0, quarter, 256):
            real, imag = [], []
            for r in range(QUAD):
                part = spectrum[r, pl.ds(top, tile), :]
                real.append(
                    jnp.dot(part, quad_ref[r, :, left : left + 256], preferred_element_type=F32)
                )
                imag.append(
                    jnp.dot(
                        part,
                        quad_ref[r, :, quarter + left : quarter + left + 256],
                        preferred_element_type=F32,
                    )
                )
            er, ei = real[0] + real[2], imag[0] + imag[2]
            fr, fi = real[0] - real[2], imag[0] - imag[2]
            gr, gi = real[1] + real[3], imag[1] + imag[3]
            hr, hi = real[1] - real[3], imag[1] - imag[3]
            parts = [
                (er + gr, ei + gi),
                (fr - hi, fi + hr),
                (er - gr, ei - gi),
                (fr + hi, fi - hr),
            ]
            for q in range(QUAD):
                for c in range(2):
                    scaled = parts[q][c] * scale_second
                    image_ref[0, c, :, q * quarter + left : q * quarter + left + 256] = scaled


def make_image(me, places, vis, pairs, table, owners):
    nblocks = places.shape[0]
    steps = nblocks // BATCH
    rows, tiles = table.shape
    band = GRID // owners
    tile = min(128, band)
    groups = COLS // 4
    cos_table, sin_table = class_tables(owners)
    before = steps + groups
    return pl.pallas_call(
        functools.partial(fused_kernel, band, tile, steps),
        out_shape=jax.ShapeDtypeStruct((1, 2, band, GRID), F32),
        grid_spec=pltpu.PrefetchScalarGridSpec(
            num_scalar_prefetch=2,
            grid=(before + band // tile,),
            in_specs=[
                pl.BlockSpec((2 * BATCH, 128), lambda i, p, m: (jnp.minimum(i, steps - 1), 0)),
                pl.BlockSpec((2 * BATCH, 128), lambda i, p, m: (jnp.minimum(i, steps - 1), 0)),
                pl.BlockSpec((rows, tiles), lambda i, p, m: (0, 0)),
                pl.BlockSpec((band, GRID // QUAD), lambda i, p, m: (m[0], 0)),
                pl.BlockSpec((band, GRID // QUAD), lambda i, p, m: (m[0], 0)),
                pl.BlockSpec(memory_space=pl.ANY),
            ],
            out_specs=pl.BlockSpec(
                (1, 2, tile, GRID), lambda i, p, m: (0, 0, jnp.maximum(i - before, 0), 0)
            ),
            scratch_shapes=[
                pltpu.VMEM((COLS, COLS, KERN, 2 * KERN), F32),
                pltpu.VMEM((tiles, BATCH * 256), BF),
                pltpu.VMEM((rows, BATCH * 256), F32),
                pltpu.VMEM((BATCH, 128, 128), BF),
                pltpu.VMEM((BATCH, 256, 128), BF),
                pltpu.VMEM((QUAD, GRID // QUAD, 512), BF),
                pltpu.VMEM((QUAD, band, 128), F32),
                pltpu.VMEM((QUAD, band, GRID // 2), BF),
                pltpu.VMEM((QUAD, GRID // 2, GRID // 2), BF),
                pltpu.SemaphoreType.DMA,
            ],
        ),
        compiler_params=pltpu.CompilerParams(vmem_limit_bytes=LIMIT),
    )(
        places, me, vis, pairs, table,
        jnp.asarray(cos_table), jnp.asarray(sin_table), jnp.asarray(quad_table()),
    )


def rounded(x):
    return lax.reduce_precision(x, exponent_bits=8, mantissa_bits=7)


def lookup_rows(beams, support, gains):
    half = beams.shape[1] // 2
    width = half // 4
    masked = beams * jnp.repeat(support, width, axis=1).astype(F32)
    by_column = masked.T
    along_u = by_column[:half].reshape(half // QUAD, QUAD, -1).transpose(1, 0, 2).reshape(half, -1)
    values = jnp.concatenate([along_u, by_column[half:]], axis=0)
    high = rounded(values)
    low = values - high
    gain_high = rounded(gains)
    rest = gains - gain_high
    gain_mid = rounded(rest)
    gain_low = rest - gain_mid
    gain_rows = jnp.stack([gain_high, gain_mid, gain_low], axis=1).reshape(6, -1)
    blank = jnp.zeros((10, gains.shape[1]), F32)
    return jnp.concatenate([high, low, gain_rows, blank], axis=0).astype(BF)


def on_device(visibilities, tile_pairs, owner_tiles, cell_ids, gains, beams, support):
    owners = lax.axis_size("uv")
    me = lax.axis_index("uv").astype(jnp.int32).reshape(1)
    nblocks, _, rows_each = visibilities.shape[1:]
    band = GRID // owners
    bands_each = band // KERN
    lines = 2 * nblocks * rows_each // 128
    meta = jnp.concatenate([owner_tiles[0, :, 0], cell_ids[0]]).reshape(-1, 128)
    meta = jnp.pad(meta, ((0, 16 - meta.shape[0]), (0, 0)))
    packed = jnp.concatenate(
        [
            visibilities.reshape(lines, 128),
            tile_pairs.reshape(lines, 128).astype(BF),
            meta.astype(BF),
        ],
        axis=0,
    )
    gathered = lax.all_gather(packed, "uv", axis=0, tiled=False)
    vis = gathered[:, :lines].reshape(owners * lines, 128).astype(F32)
    pairs = gathered[:, lines : 2 * lines].reshape(owners * lines, 128).astype(F32)
    notes = gathered[:, 2 * lines : 2 * lines + 2 * nblocks // 128].reshape(owners, 2, nblocks)
    notes = notes.astype(jnp.int32)
    cells = notes[:, 1]
    places = (cells % COLS) * COLS + notes[:, 0] * bands_each + cells // COLS
    table = lookup_rows(beams, support, gains[0])
    return make_image(me, places.reshape(-1), vis, pairs, table, owners)


def solution(mesh):
    return jax.shard_map(
        on_device,
        mesh=mesh,
        in_specs=(
            P(("groups", "chan", "pol"), "uv", None, None),
            P(("groups", "uv"), None, None),
            P(("groups", "chan", "pol"), "uv", None),
            P(("groups", "chan", "pol"), "uv"),
            P(("groups", "chan", "pol"), None, None),
            P(),
            P(),
        ),
        out_specs=P(("groups", "chan", "pol"), None, "uv", None),
        check_vma=False,
    )
```

```python
import functools
import math

import jax
import jax.numpy as jnp
import ml_dtypes
import numpy as np
from jax import lax
from jax.experimental import pallas as pl
from jax.experimental.pallas import tpu as pltpu
from jax.sharding import PartitionSpec as P

GRID = 2048
KERN = 64
COLS = GRID // KERN
QUAD = 4
BATCH = 16
LIMIT = 60 * 1024 * 1024
BF = jnp.bfloat16
F32 = jnp.float32


@functools.lru_cache(maxsize=None)
def full_tables():
    index = np.arange(GRID)
    angles = 2.0 * np.pi * ((index[:, None] * index[None, :]) % GRID) / GRID
    return (
        np.cos(angles).astype(np.float32).astype(ml_dtypes.bfloat16),
        np.sin(angles).astype(np.float32).astype(ml_dtypes.bfloat16),
    )


@functools.lru_cache(maxsize=None)
def quad_table():
    cos_table, sin_table = full_tables()
    quarter = GRID // QUAD
    rows = np.arange(GRID).reshape(COLS, KERN // QUAD, QUAD)
    out = np.zeros((QUAD, COLS, 2, KERN // QUAD, 2, quarter), ml_dtypes.bfloat16)
    for r in range(QUAD):
        c = cos_table[rows[:, :, r], :quarter]
        s = sin_table[rows[:, :, r], :quarter]
        out[r, :, 0, :, 0] = c
        out[r, :, 1, :, 0] = -s
        out[r, :, 0, :, 1] = s
        out[r, :, 1, :, 1] = c
    return out.reshape(QUAD, GRID // 2, GRID // 2)


@functools.lru_cache(maxsize=None)
def class_tables(owners):
    cos_table, sin_table = full_tables()
    band = GRID // owners
    order = np.arange(GRID).reshape(owners, band // QUAD, QUAD).transpose(0, 2, 1).reshape(-1)
    quarter = GRID // QUAD
    both = np.stack(
        [table[order, :quarter].reshape(owners, QUAD, -1, quarter) for table in (cos_table, sin_table)],
        axis=2,
    )
    return both.reshape(2 * GRID, quarter)


def fused_kernel(
    band, tile, steps,
    place_ref, me_ref, vis_ref, pair_ref, table_ref, class_ref, quad_hbm,
    image_ref,
    total, chosen, looked, left_rows, right_rows, mixed_cells, woven, spectrum, quad_ref, quad_sem,
):
    step = pl.program_id(0)
    groups = COLS // 4
    quarter = GRID // QUAD
    class_rows = band // QUAD
    scale_first = 1.0 / (16.0 * math.sqrt(GRID))
    scale_second = 1.0 / math.sqrt(GRID)
    quad_copy = pltpu.make_async_copy(quad_hbm, quad_ref, quad_sem)

    @pl.when(step == 0)
    def _():
        quad_copy.start()

        @pl.loop(0, COLS)
        def _(col):
            total[col] = jnp.zeros((COLS, KERN, 2 * KERN), F32)

    @pl.when(step < steps)
    def _():
        tiles = table_ref.shape[1]
        number = lax.broadcasted_iota(jnp.int32, (tiles, 256), 0).astype(F32).astype(BF)
        one, nil = jnp.asarray(1, BF), jnp.asarray(0, BF)
        for j in range(BATCH):
            pair = jnp.concatenate(
                [pair_ref[2 * j : 2 * j + 1, :], pair_ref[2 * j + 1 : 2 * j + 2, :]], axis=1
            )
            pair = jnp.broadcast_to(pair, (16, 256)).astype(BF)
            pair = jnp.concatenate([pair] * (tiles // 16), axis=0)
            chosen[:, j * 256 : (j + 1) * 256] = jnp.where(number == pair, one, nil)
        for j in range(0, BATCH, 2):
            looked[:, j * 256 : (j + 2) * 256] = jnp.dot(
                table_ref[...], chosen[:, j * 256 : (j + 2) * 256], preferred_element_type=F32
            )
        for j in range(BATCH):
            rows = looked[:, j * 256 : (j + 1) * 256]
            both = rows[:128] + rows[128:256]
            kernels = both[:, :128] * both[:, 128:]
            ku, kv = kernels[:64], kernels[64:]
            real = rows[256:257] + rows[258:259] + rows[260:261]
            imag = rows[257:258] + rows[259:260] + rows[261:262]
            sr, tr, si, ti = real[:, :128], real[:, 128:], imag[:, :128], imag[:, 128:]
            vr, vi = vis_ref[2 * j : 2 * j + 1, :], vis_ref[2 * j + 1 : 2 * j + 2, :]
            pr = sr * vr - si * vi
            pi = sr * vi + si * vr
            gr = pr * tr + pi * ti
            gi = pi * tr - pr * ti
            weighted = []
            for r in range(QUAD):
                part = ku[16 * r : 16 * r + 16]
                weighted += [gr * part, gi * part]
            weighted = jnp.concatenate(weighted, axis=0)
            w_high = weighted.astype(BF)
            w_low = (weighted - w_high.astype(F32)).astype(BF)
            v_high = kv.astype(BF)
            v_low = (kv - v_high.astype(F32)).astype(BF)
            left_rows[j] = jnp.concatenate([v_high, v_low], axis=0)
            right_rows[j] = jnp.concatenate([w_high, w_low], axis=0)
        for j in range(BATCH):
            product = lax.dot_general(
                left_rows[j], right_rows[j], (((1,), (1,)), ((), ())), preferred_element_type=F32
            )
            cell = product[:64, :128] + (
                product[64:, :128] + product[:64, 128:] + product[64:, 128:]
            )
            where = place_ref[step * BATCH + j]
            total[where // COLS, where % COLS] += cell

    @pl.when(step == steps)
    def _():
        quad_copy.wait()

    @pl.when((step >= steps) & (step < steps + groups))
    def _():
        group = step - steps
        far = COLS // QUAD

        @pl.loop(0, far)
        def _(col):
            top = pl.multiple_of(col * KERN, KERN)
            lane = lax.broadcasted_iota(jnp.int32, (KERN, 128), 1) % 32
            for k in range(4):
                x = [
                    total[col + far * q, group * 4 + k].astype(BF).astype(F32) for q in range(QUAD)
                ]
                e, f, g, h = x[0] + x[2], x[0] - x[2], x[1] + x[3], x[1] - x[3]
                turned = jnp.where(lane < 16, -pltpu.roll(h, 112, 1), pltpu.roll(h, 16, 1))
                for s, y in enumerate([e + g, f + turned, e - g, f - turned]):
                    mixed_cells[s, pl.ds(top, KERN), k * 128 : (k + 1) * 128] = y.astype(BF)

        lane = lax.broadcasted_iota(jnp.int32, (class_rows, 512), 1) % 32
        for s in range(QUAD):
            mine = slice(2 * s * class_rows, 2 * (s + 1) * class_rows)
            turned = jnp.dot(class_ref[mine, :], mixed_cells[s], preferred_element_type=F32)
            with_cos, with_sin = turned[:class_rows], turned[class_rows:]
            swapped = jnp.where(
                lane < 16, -pltpu.roll(with_sin, 512 - 16, 1), pltpu.roll(with_sin, 16, 1)
            )
            mixed = (with_cos + swapped) * scale_first
            for r in range(QUAD):
                picked = jnp.concatenate(
                    [mixed[:, 128 * k + 32 * r : 128 * k + 32 * r + 32] for k in range(4)], axis=1
                )
                woven[r, pl.ds(s, class_rows, stride=QUAD), :] = picked
        for r in range(QUAD):
            spectrum[r, :, pl.ds(pl.multiple_of(group * 128, 128), 128)] = woven[r].astype(BF)

    @pl.when(step >= steps + groups)
    def _():
        top = pl.multiple_of((step - steps - groups) * tile, tile)
        for left in range(0, quarter, 256):
            real, imag = [], []
            for r in range(QUAD):
                part = spectrum[r, pl.ds(top, tile), :]
                real.append(
                    jnp.dot(part, quad_ref[r, :, left : left + 256], preferred_element_type=F32)
                )
                imag.append(
                    jnp.dot(
                        part,
                        quad_ref[r, :, quarter + left : quarter + left + 256],
                        preferred_element_type=F32,
                    )
                )
            er, ei = real[0] + real[2], imag[0] + imag[2]
            fr, fi = real[0] - real[2], imag[0] - imag[2]
            gr, gi = real[1] + real[3], imag[1] + imag[3]
            hr, hi = real[1] - real[3], imag[1] - imag[3]
            parts = [
                (er + gr, ei + gi),
                (fr - hi, fi + hr),
                (er - gr, ei - gi),
                (fr + hi, fi - hr),
            ]
            for q in range(QUAD):
                for c in range(2):
                    scaled = parts[q][c] * scale_second
                    image_ref[0, c, :, q * quarter + left : q * quarter + left + 256] = scaled


def make_image(me, places, vis, pairs, table, owners):
    nblocks = places.shape[0]
    steps = nblocks // BATCH
    rows, tiles = table.shape
    band = GRID // owners
    tile = min(256, band)
    groups = COLS // 4
    before = steps + groups
    return pl.pallas_call(
        functools.partial(fused_kernel, band, tile, steps),
        out_shape=jax.ShapeDtypeStruct((1, 2, band, GRID), F32),
        grid_spec=pltpu.PrefetchScalarGridSpec(
            num_scalar_prefetch=2,
            grid=(before + band // tile,),
            in_specs=[
                pl.BlockSpec((2 * BATCH, 128), lambda i, p, m: (jnp.minimum(i, steps - 1), 0)),
                pl.BlockSpec((2 * BATCH, 128), lambda i, p, m: (jnp.minimum(i, steps - 1), 0)),
                pl.BlockSpec((rows, tiles), lambda i, p, m: (0, 0)),
                pl.BlockSpec((2 * band, GRID // QUAD), lambda i, p, m: (m[0], 0)),
                pl.BlockSpec(memory_space=pl.ANY),
            ],
            out_specs=pl.BlockSpec(
                (1, 2, tile, GRID), lambda i, p, m: (0, 0, jnp.maximum(i - before, 0), 0)
            ),
            scratch_shapes=[
                pltpu.VMEM((COLS, COLS, KERN, 2 * KERN), F32),
                pltpu.VMEM((tiles, BATCH * 256), BF),
                pltpu.VMEM((rows, BATCH * 256), F32),
                pltpu.VMEM((BATCH, 128, 128), BF),
                pltpu.VMEM((BATCH, 256, 128), BF),
                pltpu.VMEM((QUAD, GRID // QUAD, 512), BF),
                pltpu.VMEM((QUAD, band, 128), F32),
                pltpu.VMEM((QUAD, band, GRID // 2), BF),
                pltpu.VMEM((QUAD, GRID // 2, GRID // 2), BF),
                pltpu.SemaphoreType.DMA,
            ],
        ),
        compiler_params=pltpu.CompilerParams(vmem_limit_bytes=LIMIT),
    )(
        places, me, vis, pairs, table,
        jnp.asarray(class_tables(owners)), jnp.asarray(quad_table()),
    )


@functools.lru_cache(maxsize=None)
def row_order():
    order = np.concatenate(
        [np.arange(KERN).reshape(-1, QUAD).T.reshape(-1), KERN + np.arange(KERN)]
    )
    return np.eye(2 * KERN, dtype=np.float32)[order].astype(ml_dtypes.bfloat16)


def gather_kernel(
    n, lines,
    vis_ref, pair_ref, meta_ref, beams_ref, support_ref, gains_ref, order_ref,
    vis_out, pair_out, meta_out, table_out,
    packed, slots, send_sem, recv_sem,
):
    me = lax.axis_index("uv")
    others = [lax.rem(me + o, n) for o in range(1, n)]
    barrier = pltpu.get_barrier_semaphore()
    for other in others:
        pl.semaphore_signal(
            barrier, inc=1, device_id={"uv": other}, device_id_type=pl.DeviceIdType.MESH
        )
    packed[:lines] = vis_ref[...]
    packed[lines : 2 * lines] = pair_ref[...].astype(F32).astype(BF)
    packed[2 * lines :] = meta_ref[...].astype(F32).astype(BF)
    pl.semaphore_wait(barrier, n - 1)
    copies = []
    for o, other in enumerate(others):
        copy = pltpu.make_async_remote_copy(
            src_ref=packed,
            dst_ref=slots.at[me],
            send_sem=send_sem.at[o],
            recv_sem=recv_sem.at[o],
            device_id={"uv": other},
            device_id_type=pl.DeviceIdType.MESH,
        )
        copy.start()
        copies.append(copy)
    slots[me] = packed[...]
    lane = lax.broadcasted_iota(jnp.int32, beams_ref.shape, 1) // (KERN // 4)
    support = support_ref[...].astype(F32)
    mask = jnp.zeros(beams_ref.shape, F32)
    for k in range(8):
        mask = jnp.where(lane == k, support[:, k : k + 1], mask)
    masked = beams_ref[...] * mask
    high = masked.astype(BF)
    low = (masked - high.astype(F32)).astype(BF)
    across = (((1,), (1,)), ((), ()))
    for k, part in enumerate([high, low]):
        table_out[k * 128 : (k + 1) * 128] = lax.dot_general(
            order_ref[...], part, across, preferred_element_type=F32
        ).astype(BF)
    gains = gains_ref[...]
    gain_high = gains.astype(BF).astype(F32)
    rest = gains - gain_high
    gain_mid = rest.astype(BF).astype(F32)
    blank = jnp.zeros((10, gains.shape[1]), F32)
    table_out[256:] = jnp.concatenate([gain_high, gain_mid, rest - gain_mid, blank], axis=0).astype(
        BF
    )
    for copy in copies:
        copy.wait()
    for i in range(n):
        vis_out[i * lines : (i + 1) * lines] = slots[i, :lines].astype(F32)
        pair_out[i * lines : (i + 1) * lines] = slots[i, lines : 2 * lines].astype(F32)
        meta_out[i] = slots[i, 2 * lines :].astype(F32).astype(jnp.int32)


def gather(n, vis, pairs, meta, beams, support, gains):
    lines = vis.shape[0]
    extra = meta.shape[0]
    tiles = beams.shape[0]
    vmem = pl.BlockSpec(memory_space=pltpu.VMEM)
    return pl.pallas_call(
        functools.partial(gather_kernel, n, lines),
        out_shape=(
            jax.ShapeDtypeStruct((n * lines, 128), F32),
            jax.ShapeDtypeStruct((n * lines, 128), F32),
            jax.ShapeDtypeStruct((n, extra, 128), jnp.int32),
            jax.ShapeDtypeStruct((272, tiles), BF),
        ),
        in_specs=[vmem] * 7,
        out_specs=(vmem,) * 4,
        scratch_shapes=[
            pltpu.VMEM((2 * lines + extra, 128), BF),
            pltpu.VMEM((n, 2 * lines + extra, 128), BF),
            pltpu.SemaphoreType.DMA((n - 1,)),
            pltpu.SemaphoreType.DMA((n - 1,)),
        ],
        compiler_params=pltpu.CompilerParams(
            collective_id=0, has_side_effects=True, vmem_limit_bytes=32 * 1024 * 1024
        ),
    )(vis, pairs, meta, beams, support, gains, jnp.asarray(row_order()))


def on_device(visibilities, tile_pairs, owner_tiles, cell_ids, gains, beams, support):
    owners = lax.axis_size("uv")
    me = lax.axis_index("uv").astype(jnp.int32).reshape(1)
    nblocks, _, rows_each = visibilities.shape[1:]
    bands_each = GRID // owners // KERN
    lines = 2 * nblocks * rows_each // 128
    meta = jnp.concatenate([owner_tiles[0, :, 0], cell_ids[0]]).reshape(-1, 128)
    noted = meta.shape[0]
    meta = jnp.pad(meta, ((0, 16 - noted), (0, 0)))
    vis, pairs, notes, table = gather(
        owners,
        visibilities.reshape(lines, 128),
        tile_pairs.reshape(lines, 128),
        meta,
        beams,
        support,
        gains[0],
    )
    notes = notes[:, :noted].reshape(owners, 2, nblocks)
    cells = notes[:, 1]
    places = (cells % COLS) * COLS + notes[:, 0] * bands_each + cells // COLS
    return make_image(me, places.reshape(-1), vis, pairs, table, owners)


def solution(mesh):
    return jax.shard_map(
        on_device,
        mesh=mesh,
        in_specs=(
            P(("groups", "chan", "pol"), "uv", None, None),
            P(("groups", "uv"), None, None),
            P(("groups", "chan", "pol"), "uv", None),
            P(("groups", "chan", "pol"), "uv"),
            P(("groups", "chan", "pol"), None, None),
            P(),
            P(),
        ),
        out_specs=P(("groups", "chan", "pol"), None, "uv", None),
        check_vma=False,
    )
```

```python
import functools
import math

import jax
import jax.numpy as jnp
import ml_dtypes
import numpy as np
from jax import lax
from jax.experimental import pallas as pl
from jax.experimental.pallas import tpu as pltpu
from jax.sharding import PartitionSpec as P

GRID = 2048
KERN = 64
COLS = GRID // KERN
QUAD = 4
BATCH = 16
LIMIT = 60 * 1024 * 1024
BF = jnp.bfloat16
F32 = jnp.float32


@functools.lru_cache(maxsize=None)
def full_tables():
    index = np.arange(GRID)
    angles = 2.0 * np.pi * ((index[:, None] * index[None, :]) % GRID) / GRID
    return (
        np.cos(angles).astype(np.float32).astype(ml_dtypes.bfloat16),
        np.sin(angles).astype(np.float32).astype(ml_dtypes.bfloat16),
    )


@functools.lru_cache(maxsize=None)
def quad_table():
    cos_table, sin_table = full_tables()
    quarter = GRID // QUAD
    rows = np.arange(GRID).reshape(COLS, KERN // QUAD, QUAD)
    out = np.zeros((QUAD, COLS, 2, KERN // QUAD, 2, quarter), ml_dtypes.bfloat16)
    for r in range(QUAD):
        c = cos_table[rows[:, :, r], :quarter]
        s = sin_table[rows[:, :, r], :quarter]
        out[r, :, 0, :, 0] = c
        out[r, :, 1, :, 0] = -s
        out[r, :, 0, :, 1] = s
        out[r, :, 1, :, 1] = c
    return out.reshape(QUAD, GRID // 2, GRID // 2)


@functools.lru_cache(maxsize=None)
def class_tables(owners):
    cos_table, sin_table = full_tables()
    band = GRID // owners
    order = np.arange(GRID).reshape(owners, band // QUAD, QUAD).transpose(0, 2, 1).reshape(-1)
    quarter = GRID // QUAD
    both = np.stack(
        [table[order, :quarter].reshape(owners, QUAD, -1, quarter) for table in (cos_table, sin_table)],
        axis=2,
    )
    return both.reshape(2 * GRID, quarter)


def fused_kernel(
    band, tile, steps,
    place_ref, me_ref, vis_ref, pair_ref, table_ref, class_ref, quad_hbm,
    image_ref,
    total, chosen, looked, left_rows, right_rows, mixed_cells, woven, spectrum, quad_ref, quad_sem,
):
    step = pl.program_id(0)
    groups = COLS // 4
    quarter = GRID // QUAD
    class_rows = band // QUAD
    scale_first = 1.0 / (16.0 * math.sqrt(GRID))
    scale_second = 1.0 / math.sqrt(GRID)
    quad_copy = pltpu.make_async_copy(quad_hbm, quad_ref, quad_sem)

    @pl.when(step == 0)
    def _():
        quad_copy.start()

        @pl.loop(0, COLS)
        def _(col):
            total[col] = jnp.zeros((COLS, KERN, 2 * KERN), F32)

    @pl.when(step < steps)
    def _():
        tiles = table_ref.shape[1]
        number = lax.broadcasted_iota(jnp.int32, (tiles, 256), 0).astype(F32).astype(BF)
        one, nil = jnp.asarray(1, BF), jnp.asarray(0, BF)
        for j in range(BATCH):
            pair = jnp.concatenate(
                [pair_ref[2 * j : 2 * j + 1, :], pair_ref[2 * j + 1 : 2 * j + 2, :]], axis=1
            )
            pair = jnp.broadcast_to(pair, (16, 256)).astype(BF)
            pair = jnp.concatenate([pair] * (tiles // 16), axis=0)
            chosen[:, j * 256 : (j + 1) * 256] = jnp.where(number == pair, one, nil)
        for j in range(0, BATCH, 2):
            looked[:, j * 256 : (j + 2) * 256] = jnp.dot(
                table_ref[...], chosen[:, j * 256 : (j + 2) * 256], preferred_element_type=F32
            )
        for j in range(BATCH):
            rows = looked[:, j * 256 : (j + 1) * 256]
            both = rows[:128] + rows[128:256]
            kernels = both[:, :128] * both[:, 128:]
            ku, kv = kernels[:64], kernels[64:]
            real = rows[256:257] + rows[258:259] + rows[260:261]
            imag = rows[257:258] + rows[259:260] + rows[261:262]
            sr, tr, si, ti = real[:, :128], real[:, 128:], imag[:, :128], imag[:, 128:]
            vr, vi = vis_ref[2 * j : 2 * j + 1, :], vis_ref[2 * j + 1 : 2 * j + 2, :]
            pr = sr * vr - si * vi
            pi = sr * vi + si * vr
            gr = pr * tr + pi * ti
            gi = pi * tr - pr * ti
            weighted = []
            for r in range(QUAD):
                part = ku[16 * r : 16 * r + 16]
                weighted += [gr * part, gi * part]
            weighted = jnp.concatenate(weighted, axis=0)
            w_high = weighted.astype(BF)
            w_low = (weighted - w_high.astype(F32)).astype(BF)
            v_high = kv.astype(BF)
            v_low = (kv - v_high.astype(F32)).astype(BF)
            left_rows[j] = jnp.concatenate([v_high, v_low], axis=0)
            right_rows[j] = jnp.concatenate([w_high, w_low], axis=0)
        for j in range(BATCH):
            product = lax.dot_general(
                left_rows[j], right_rows[j], (((1,), (1,)), ((), ())), preferred_element_type=F32
            )
            cell = product[:64, :128] + (
                product[64:, :128] + product[:64, 128:] + product[64:, 128:]
            )
            where = place_ref[step * BATCH + j]
            total[where // COLS, where % COLS] += cell

    @pl.when(step == steps)
    def _():
        quad_copy.wait()

    @pl.when((step >= steps) & (step < steps + groups))
    def _():
        group = step - steps
        far = COLS // QUAD

        @pl.loop(0, far)
        def _(col):
            top = pl.multiple_of(col * KERN, KERN)
            lane = lax.broadcasted_iota(jnp.int32, (KERN, 128), 1) % 32
            for k in range(4):
                x = [
                    total[col + far * q, group * 4 + k].astype(BF).astype(F32) for q in range(QUAD)
                ]
                e, f, g, h = x[0] + x[2], x[0] - x[2], x[1] + x[3], x[1] - x[3]
                turned = jnp.where(lane < 16, -pltpu.roll(h, 112, 1), pltpu.roll(h, 16, 1))
                for s, y in enumerate([e + g, f + turned, e - g, f - turned]):
                    mixed_cells[s, pl.ds(top, KERN), k * 128 : (k + 1) * 128] = y.astype(BF)

        lane = lax.broadcasted_iota(jnp.int32, (class_rows, 512), 1) % 32
        for s in range(QUAD):
            mine = slice(2 * s * class_rows, 2 * (s + 1) * class_rows)
            turned = jnp.dot(class_ref[mine, :], mixed_cells[s], preferred_element_type=F32)
            with_cos, with_sin = turned[:class_rows], turned[class_rows:]
            swapped = jnp.where(
                lane < 16, -pltpu.roll(with_sin, 512 - 16, 1), pltpu.roll(with_sin, 16, 1)
            )
            mixed = (with_cos + swapped) * scale_first
            for r in range(QUAD):
                picked = jnp.concatenate(
                    [mixed[:, 128 * k + 32 * r : 128 * k + 32 * r + 32] for k in range(4)], axis=1
                )
                woven[r, pl.ds(s, class_rows, stride=QUAD), :] = picked
        for r in range(QUAD):
            spectrum[r, :, pl.ds(pl.multiple_of(group * 128, 128), 128)] = woven[r].astype(BF)

    @pl.when(step >= steps + groups)
    def _():
        top = pl.multiple_of((step - steps - groups) * tile, tile)
        for left in range(0, quarter, 256):
            real, imag = [], []
            for r in range(QUAD):
                part = spectrum[r, pl.ds(top, tile), :]
                real.append(
                    jnp.dot(part, quad_ref[r, :, left : left + 256], preferred_element_type=F32)
                )
                imag.append(
                    jnp.dot(
                        part,
                        quad_ref[r, :, quarter + left : quarter + left + 256],
                        preferred_element_type=F32,
                    )
                )
            er, ei = real[0] + real[2], imag[0] + imag[2]
            fr, fi = real[0] - real[2], imag[0] - imag[2]
            gr, gi = real[1] + real[3], imag[1] + imag[3]
            hr, hi = real[1] - real[3], imag[1] - imag[3]
            parts = [
                (er + gr, ei + gi),
                (fr - hi, fi + hr),
                (er - gr, ei - gi),
                (fr + hi, fi - hr),
            ]
            for q in range(QUAD):
                for c in range(2):
                    scaled = parts[q][c] * scale_second
                    image_ref[0, c, :, q * quarter + left : q * quarter + left + 256] = scaled


def make_image(me, places, vis, pairs, table, owners):
    nblocks = places.shape[0]
    steps = nblocks // BATCH
    rows, tiles = table.shape
    band = GRID // owners
    tile = min(256, band)
    groups = COLS // 4
    before = steps + groups
    return pl.pallas_call(
        functools.partial(fused_kernel, band, tile, steps),
        out_shape=jax.ShapeDtypeStruct((1, 2, band, GRID), F32),
        grid_spec=pltpu.PrefetchScalarGridSpec(
            num_scalar_prefetch=2,
            grid=(before + band // tile,),
            in_specs=[
                pl.BlockSpec((2 * BATCH, 128), lambda i, p, m: (jnp.minimum(i, steps - 1), 0)),
                pl.BlockSpec((2 * BATCH, 128), lambda i, p, m: (jnp.minimum(i, steps - 1), 0)),
                pl.BlockSpec((rows, tiles), lambda i, p, m: (0, 0)),
                pl.BlockSpec((2 * band, GRID // QUAD), lambda i, p, m: (m[0], 0)),
                pl.BlockSpec(memory_space=pl.ANY),
            ],
            out_specs=pl.BlockSpec(
                (1, 2, tile, GRID), lambda i, p, m: (0, 0, jnp.maximum(i - before, 0), 0)
            ),
            scratch_shapes=[
                pltpu.VMEM((COLS, COLS, KERN, 2 * KERN), F32),
                pltpu.VMEM((tiles, BATCH * 256), BF),
                pltpu.VMEM((rows, BATCH * 256), F32),
                pltpu.VMEM((BATCH, 128, 128), BF),
                pltpu.VMEM((BATCH, 256, 128), BF),
                pltpu.VMEM((QUAD, GRID // QUAD, 512), BF),
                pltpu.VMEM((QUAD, band, 128), F32),
                pltpu.VMEM((QUAD, band, GRID // 2), BF),
                pltpu.VMEM((QUAD, GRID // 2, GRID // 2), BF),
                pltpu.SemaphoreType.DMA,
            ],
        ),
        compiler_params=pltpu.CompilerParams(vmem_limit_bytes=LIMIT),
    )(
        places, me, vis, pairs, table,
        jnp.asarray(class_tables(owners)), jnp.asarray(quad_table()),
    )


@functools.lru_cache(maxsize=None)
def row_order():
    order = np.concatenate(
        [np.arange(KERN).reshape(-1, QUAD).T.reshape(-1), KERN + np.arange(KERN)]
    )
    return np.eye(2 * KERN, dtype=np.float32)[order].astype(ml_dtypes.bfloat16)


def gather_kernel(
    n, lines,
    vis_ref, pair_ref, meta_ref, beams_ref, support_ref, gains_ref, order_ref,
    vis_out, pair_out, meta_out, table_out,
    packed, slots, send_sem, recv_sem,
):
    me = lax.axis_index("uv")
    others = [lax.rem(me + o, n) for o in range(1, n)]
    barrier = pltpu.get_barrier_semaphore()
    for other in others:
        pl.semaphore_signal(
            barrier, inc=1, device_id={"uv": other}, device_id_type=pl.DeviceIdType.MESH
        )
    packed[:lines] = vis_ref[...]
    packed[lines : 2 * lines] = pair_ref[...].astype(F32).astype(BF)
    packed[2 * lines :] = meta_ref[...].astype(F32).astype(BF)
    pl.semaphore_wait(barrier, n - 1)
    copies = []
    for o, other in enumerate(others):
        copy = pltpu.make_async_remote_copy(
            src_ref=packed,
            dst_ref=slots.at[me],
            send_sem=send_sem.at[o],
            recv_sem=recv_sem.at[o],
            device_id={"uv": other},
            device_id_type=pl.DeviceIdType.MESH,
        )
        copy.start()
        copies.append(copy)
    slots[me] = packed[...]
    lane = lax.broadcasted_iota(jnp.int32, beams_ref.shape, 1) // (KERN // 4)
    support = support_ref[...].astype(F32)
    mask = jnp.zeros(beams_ref.shape, F32)
    for k in range(8):
        mask = jnp.where(lane == k, support[:, k : k + 1], mask)
    masked = beams_ref[...] * mask
    high = masked.astype(BF)
    low = (masked - high.astype(F32)).astype(BF)
    across = (((1,), (1,)), ((), ()))
    for k, part in enumerate([high, low]):
        table_out[k * 128 : (k + 1) * 128] = lax.dot_general(
            order_ref[...], part, across, preferred_element_type=F32
        ).astype(BF)
    gains = gains_ref[...]
    gain_high = gains.astype(BF).astype(F32)
    rest = gains - gain_high
    gain_mid = rest.astype(BF).astype(F32)
    blank = jnp.zeros((10, gains.shape[1]), F32)
    table_out[256:] = jnp.concatenate([gain_high, gain_mid, rest - gain_mid, blank], axis=0).astype(
        BF
    )
    for copy in copies:
        copy.wait()
    for i in range(n):
        vis_out[i * lines : (i + 1) * lines] = slots[i, :lines].astype(F32)
        pair_out[i * lines : (i + 1) * lines] = slots[i, lines : 2 * lines].astype(F32)
        meta_out[i] = slots[i, 2 * lines :].astype(F32).astype(jnp.int32)


def gather(n, vis, pairs, meta, beams, support, gains):
    lines = vis.shape[0]
    extra = meta.shape[0]
    tiles = beams.shape[0]
    operands = (vis, pairs, meta, beams, support, gains, jnp.asarray(row_order()))
    return pl.pallas_call(
        functools.partial(gather_kernel, n, lines),
        grid=(1,),
        out_shape=(
            jax.ShapeDtypeStruct((n * lines, 128), F32),
            jax.ShapeDtypeStruct((n * lines, 128), F32),
            jax.ShapeDtypeStruct((n, extra, 128), jnp.int32),
            jax.ShapeDtypeStruct((272, tiles), BF),
        ),
        in_specs=[pl.BlockSpec(x.shape, lambda i: (0, 0)) for x in operands],
        out_specs=(
            pl.BlockSpec((n * lines, 128), lambda i: (0, 0)),
            pl.BlockSpec((n * lines, 128), lambda i: (0, 0)),
            pl.BlockSpec((n, extra, 128), lambda i: (0, 0, 0)),
            pl.BlockSpec((272, tiles), lambda i: (0, 0)),
        ),
        scratch_shapes=[
            pltpu.VMEM((2 * lines + extra, 128), BF),
            pltpu.VMEM((n, 2 * lines + extra, 128), BF),
            pltpu.SemaphoreType.DMA((n - 1,)),
            pltpu.SemaphoreType.DMA((n - 1,)),
        ],
        compiler_params=pltpu.CompilerParams(
            collective_id=0, has_side_effects=True, vmem_limit_bytes=32 * 1024 * 1024
        ),
    )(*operands)


def on_device(visibilities, tile_pairs, owner_tiles, cell_ids, gains, beams, support):
    owners = lax.axis_size("uv")
    me = lax.axis_index("uv").astype(jnp.int32).reshape(1)
    nblocks, _, rows_each = visibilities.shape[1:]
    bands_each = GRID // owners // KERN
    lines = 2 * nblocks * rows_each // 128
    meta = jnp.concatenate([owner_tiles[0, :, 0], cell_ids[0]]).reshape(-1, 128)
    noted = meta.shape[0]
    meta = jnp.pad(meta, ((0, 16 - noted), (0, 0)))
    vis, pairs, notes, table = gather(
        owners,
        visibilities.reshape(lines, 128),
        tile_pairs.reshape(lines, 128),
        meta,
        beams,
        support,
        gains[0],
    )
    notes = notes[:, :noted].reshape(owners, 2, nblocks)
    cells = notes[:, 1]
    places = (cells % COLS) * COLS + notes[:, 0] * bands_each + cells // COLS
    return make_image(me, places.reshape(-1), vis, pairs, table, owners)


def solution(mesh):
    return jax.shard_map(
        on_device,
        mesh=mesh,
        in_specs=(
            P(("groups", "chan", "pol"), "uv", None, None),
            P(("groups", "uv"), None, None),
            P(("groups", "chan", "pol"), "uv", None),
            P(("groups", "chan", "pol"), "uv"),
            P(("groups", "chan", "pol"), None, None),
            P(),
            P(),
        ),
        out_specs=P(("groups", "chan", "pol"), None, "uv", None),
        check_vma=False,
    )
```
